32 devices in a mesh: mem: 4 (over y, x), grid: 8 (over z, core).
Axes of the slice: x: 2, y: 2, z: 4, core: 2. Of those that a mesh axis runs over, the one named last changes fastest.
Arguments:
- ens_state: bfloat16 [80, 128, 512], P('mem', 'grid'), may hold values from -6 to 6
- obs_prior: bfloat16 [80, 3072, 128], P('mem', 'grid'), may hold values from -6 to 6
- obs_value: float32 [3072, 128], P('grid'), may hold values from -6 to 6
- obs_prec: float32 [3072, 128], P('grid'), may hold values from 0.01 to 0.2
- obs_len: int32 [3072], P('grid'), may hold values from 1 to 128, as said below
- pair_block: int32 [128, 256], P('grid'), may hold values from 0 to 3071, as said below
- obs_pos: float32 [3072, 128], P('grid'), may hold values from 0 to 128, as said below
Outputs:
- analysis: bfloat16 [80, 128, 512], P('mem', 'grid')
The draws below stay inside these ranges and needn't reach their ends.
Inputs may be any that keep to these rules, and one draw needn't show every extreme that they name: `obs_len`: count of valid slots of each observation block; slots at or past it are padding. Row b lists 256 distinct observation blocks; for each, pair_block[b,p] // 384 - b // 16 is -1, 0 or 1 modulo 3072 // 384. `obs_pos`: positions along the cyclic band of 128 state blocks.
All inputs are finite; a program needn't handle non-finite values. Where the reference program divides by a largest or mean magnitude, that divisor is 1e-20 or more.
Results may differ from the reference program's by a relative error of at most 0.0058.
Values may be sent and summed in bfloat16 or wider, within the bound.
A program may use at most 128 MiB of HBM per device.

```python
import math
import jax
import jax.numpy as jnp
from jax import lax

K = 80
OW = 128
NB_DEV = 16
OB_DEV = 384
P_SIZE = 256
NSIT = 3
L = 512
NB = 128
NOB = 3072
LOCR = 8


def draw_obs_len(key, part):
    counts = jax.random.randint(key, (NOB,), 1, OW + 1, dtype=jnp.int32)
    spot = jax.random.randint(jax.random.fold_in(key, 7), (), 0, NOB, dtype=jnp.int32)
    return counts.at[spot].set(OW)


def draw_pair_block(key, part):
    blocks = jnp.arange(NB, dtype=jnp.int32)
    home = blocks // NB_DEV
    keys = jax.random.split(jax.random.fold_in(key, 11), NB)
    picks = jax.vmap(lambda one: jax.random.permutation(one, 3 * OB_DEV)[:P_SIZE])(keys).astype(jnp.int32)
    return ((home[:, None] - 1) * OB_DEV + picks) % NOB


def draw_obs_pos(key, part):
    frac = jax.random.uniform(jax.random.fold_in(key, 13), (NOB, OW), jnp.float32)
    start = jnp.arange(NOB, dtype=jnp.float32)[:, None]
    return (start + frac) * (NB / NOB)


def steps_of(own_key, shape, cuts, least, top_value):
    loudness = 1.0
    for dim, parts in cuts:
        steps = jax.random.uniform(jax.random.fold_in(jax.random.fold_in(own_key, 6), dim), (parts,), jnp.float32, least / len(cuts), top_value / len(cuts))
        loudness = loudness * jnp.repeat(jnp.exp(steps), shape[dim] // parts).reshape((-1,) + (1,) * (len(shape) - 1 - dim))
    return loudness


def scatter_about(own_key, dims, scale, most, pieces=(), kind=jnp.bfloat16):
    gain = steps_of(own_key, dims, pieces, -0.22, 0.18) if pieces else 1.0
    entries = jax.random.normal(own_key, dims, jnp.float32) * scale * gain
    return jnp.minimum(jnp.maximum(entries, -most), most).astype(kind)


def setup_inputs(seed: int = 0) -> dict:
    seeds = jax.random.split(jax.random.key(seed), 8)
    return {
        "ens_state": scatter_about(seeds[0], (K, NB, L), 1.0, 6.0, ((0, 4), (1, 8))),
        "obs_prior": scatter_about(seeds[1], (K, NOB, OW), 1.0, 6.0, ((0, 4), (1, 8))),
        "obs_value": scatter_about(seeds[2], (NOB, OW), 1.0, 6.0, ((0, 8),), jnp.float32),
        "obs_prec": jnp.clip(jnp.exp(math.log(0.2) - 2.9957323 * jax.random.uniform(seeds[3], (NOB, OW), jnp.float32) ** steps_of(seeds[3], (NOB, OW), ((0, 8),), -0.2, 0.2)), 0.01, 0.2),
        "obs_len": draw_obs_len(jax.random.fold_in(seeds[7], 71), 0),
        "pair_block": draw_pair_block(jax.random.fold_in(seeds[7], 71), 0),
        "obs_pos": draw_obs_pos(jax.random.fold_in(seeds[7], 71), 0),
    }


inflation = 1.1

def finish(gram_matrix, forcing):
    members = gram_matrix.shape[0]
    highest = lax.Precision.HIGHEST
    identity = jnp.eye(members, dtype=jnp.float32)
    system = gram_matrix + (members - 1) / inflation * identity
    bound_sum = jnp.max(lax.optimization_barrier(jnp.sum(jnp.abs(system), axis=1)))
    y_iter = system / bound_sum
    z_iter = identity
    for sweep in range(NSIT):
        factor = 1.5 * identity - 0.5 * jnp.dot(z_iter, y_iter, precision=highest)
        y_iter = jnp.dot(y_iter, factor, precision=highest)
        z_iter = jnp.dot(factor, z_iter, precision=highest)
    root_inv = z_iter / jnp.sqrt(bound_sum)
    mean_weight = jnp.dot(root_inv, jnp.dot(root_inv, forcing, precision=highest), precision=highest)
    return (math.sqrt(members - 1) * root_inv + mean_weight[:, None]).astype(jnp.bfloat16)

def block_transform(perturb, departure, obs_prec, obs_pos, block_ids, center, nb_total):
    highest = lax.Precision.HIGHEST
    chosen = jnp.take(perturb, block_ids, axis=1)
    position = jnp.take(obs_pos, block_ids, axis=0)
    distance = jnp.abs(position - center)
    distance = jnp.minimum(distance, nb_total - distance)
    relative = distance / LOCR
    weight = jnp.take(obs_prec, block_ids, axis=0) * jnp.exp(-0.5 * relative * relative)
    scaled = (chosen.astype(jnp.float32) * weight).astype(jnp.bfloat16)
    gram_matrix = jnp.einsum('ipk,jpk->ij', scaled.astype(jnp.float32), chosen.astype(jnp.float32), precision=highest)
    forcing = jnp.einsum('ipk,pk->i', scaled.astype(jnp.float32), jnp.take(departure, block_ids, axis=0), precision=highest)
    return finish(gram_matrix, forcing)

def reference(ens_state, obs_prior, obs_value, obs_prec, obs_len, pair_block, obs_pos):
    members = ens_state.shape[0]
    nb_total = ens_state.shape[1]
    obs_mean = lax.optimization_barrier(jnp.sum(obs_prior, axis=0, dtype=jnp.float32)) / members
    valid = lax.broadcasted_iota(jnp.int32, obs_mean.shape, 1) < obs_len[:, None]
    perturb = jnp.where(valid, obs_prior.astype(jnp.float32) - obs_mean, 0.0).astype(jnp.bfloat16)
    departure = jnp.where(valid, obs_value - obs_mean, 0.0)
    state_mean = lax.optimization_barrier(jnp.sum(ens_state, axis=0, dtype=jnp.float32)) / members
    deviation = (ens_state.astype(jnp.float32) - state_mean).astype(jnp.bfloat16)
    centers = jnp.arange(nb_total, dtype=jnp.float32) + 0.5

    def one_block(items):
        return block_transform(perturb, departure, obs_prec, obs_pos, items[0], items[1], nb_total)
    transforms = lax.map(one_block, (pair_block, centers))

    def one_update(items):
        return jnp.einsum('il,ij->jl', items[0].astype(jnp.float32), items[1].astype(jnp.float32), precision=lax.Precision.HIGHEST)
    moved = lax.map(one_update, (jnp.transpose(deviation, (1, 0, 2)), transforms))
    return (state_mean[None, :, :] + jnp.transpose(moved, (1, 0, 2))).astype(jnp.bfloat16)
```

```python
import functools
import math

import jax
import jax.numpy as jnp
from jax import lax
from jax.experimental import pallas as pl
from jax.experimental.pallas import tpu as pltpu
from jax.sharding import PartitionSpec as P

NSIT = 3
LOCR = 8
inflation = 1.1

LANES = 128
ROWS = 16
GROUP = 8
MESH = pl.DeviceIdType.MESH
HIGHEST = lax.Precision.HIGHEST


def kernel(
    dims,
    ens_ref, obs_ref, aux_ref, pair_ref,
    out_ref,
    prior, dev, weight, aux, pairs, scaled, gram, near_send, near_recv,
    share_send, share_recv, ens_all, result,
    local_sem, obs_send, obs_recv, ens_send, ens_recv, pair_send, pair_recv,
    near_ssem, near_rsem, share_ssem, share_rsem, out_ssem, out_rsem,
):
    peers, ring, part, chunks, owned, blocks, members, pad, extra = dims
    mem = lax.axis_index("mem")
    grid = lax.axis_index("grid")
    left = lax.rem(grid + ring - 1, ring)
    right = lax.rem(grid + 1, ring)
    share = chunks * ROWS
    nb_total = blocks * ring
    obs_dev_blocks = share * peers
    slots = obs_ref.shape[2]

    def peer(step):
        return lax.rem(mem + step, peers)

    def at_peer(step):
        return (peer(step), grid)

    def obs_copy(chunk, step):
        return pltpu.make_async_remote_copy(
            src_ref=obs_ref.at[:, pl.ds(peer(step) * share + chunk * ROWS, ROWS), :],
            dst_ref=prior.at[chunk, pl.ds(mem * part, part)],
            send_sem=obs_send.at[chunk, step - 1],
            recv_sem=obs_recv.at[chunk, step - 1],
            device_id=at_peer(step),
            device_id_type=MESH,
        )

    def obs_own(chunk):
        return pltpu.make_async_copy(
            obs_ref.at[:, pl.ds(mem * share + chunk * ROWS, ROWS), :],
            prior.at[chunk, pl.ds(mem * part, part)],
            local_sem.at[2 + chunk],
        )

    def ens_copy(step):
        return pltpu.make_async_remote_copy(
            src_ref=ens_ref.at[pl.ds(peer(step) * owned, owned)],
            dst_ref=ens_all.at[mem],
            send_sem=ens_send.at[step - 1],
            recv_sem=ens_recv.at[step - 1],
            device_id=at_peer(step),
            device_id_type=MESH,
        )

    def pair_copy(side):
        return pltpu.make_async_remote_copy(
            src_ref=pair_ref,
            dst_ref=pairs.at[2 - 2 * side],
            send_sem=pair_send.at[side],
            recv_sem=pair_recv.at[side],
            device_id=(mem, left if side == 0 else right),
            device_id_type=MESH,
        )

    def near_copy(side):
        return pltpu.make_async_remote_copy(
            src_ref=near_send.at[side],
            dst_ref=near_recv.at[side],
            send_sem=near_ssem.at[side],
            recv_sem=near_rsem.at[side],
            device_id=(mem, left if side == 0 else right),
            device_id_type=MESH,
        )

    def share_copy(step):
        return pltpu.make_async_remote_copy(
            src_ref=share_send.at[peer(step)],
            dst_ref=share_recv.at[step - 1],
            send_sem=share_ssem.at[step - 1],
            recv_sem=share_rsem.at[step - 1],
            device_id=at_peer(step),
            device_id_type=MESH,
        )

    def out_copy(step):
        return pltpu.make_async_remote_copy(
            src_ref=result.at[peer(step)],
            dst_ref=out_ref.at[pl.ds(mem * owned, owned)],
            send_sem=out_ssem.at[step - 1],
            recv_sem=out_rsem.at[step - 1],
            device_id=at_peer(step),
            device_id_type=MESH,
        )

    aux_own = pltpu.make_async_copy(
        aux_ref.at[:, pl.ds(mem * share, share), :], aux, local_sem.at[0]
    )
    ens_own = pltpu.make_async_copy(
        ens_ref.at[pl.ds(mem * owned, owned)], ens_all.at[mem], local_sem.at[1]
    )
    pair_own = pltpu.make_async_copy(pair_ref, pairs.at[1], local_sem.at[2 + chunks])
    aux_own.start()
    ens_own.start()
    pair_own.start()
    for chunk in range(chunks):
        obs_own(chunk).start()

    barrier = pltpu.get_barrier_semaphore()
    for step in range(1, peers):
        pl.semaphore_signal(barrier, inc=1, device_id=at_peer(step), device_id_type=MESH)
    for side in (left, right):
        pl.semaphore_signal(barrier, inc=1, device_id=(mem, side), device_id_type=MESH)
    pl.semaphore_wait(barrier, peers + 1)

    for side in range(2):
        pair_copy(side).start()
    for chunk in range(chunks):
        for step in range(1, peers):
            obs_copy(chunk, step).start()
    for step in range(1, peers):
        ens_copy(step).start()

    aux_own.wait()
    pair_own.wait()
    for side in range(2):
        pair_copy(side).wait()

    first_block = grid * obs_dev_blocks + mem * share

    def weigh(block, _):
        third = block // blocks
        home = lax.rem(grid + third + ring - 1, ring)
        inner = block - third * blocks
        center = (home * blocks + inner).astype(jnp.float32) + 0.5
        ids = lax.broadcasted_iota(jnp.int32, (share, pairs.shape[2]), 0) + first_block
        listed = pairs[third, pl.ds(inner, 1), :] == ids
        chosen = jnp.max(listed.astype(jnp.float32), axis=1, keepdims=True)
        distance = jnp.abs(aux[2] - center)
        distance = jnp.minimum(distance, nb_total - distance)
        relative = distance / LOCR
        value = aux[1] * jnp.exp(-0.5 * relative * relative)
        weight[block] = (value * chosen).reshape(chunks, ROWS, slots)
        return 0

    lax.fori_loop(0, 3 * blocks, weigh, 0)

    def perturb(chunk):
        obs_own(chunk).wait()
        for step in range(1, peers):
            obs_copy(chunk, step).wait()
        values = prior[chunk].astype(jnp.float32)
        mean = jnp.sum(values, axis=0) / members
        rows = pl.ds(pl.multiple_of(chunk * ROWS, ROWS), ROWS)
        slot = lax.broadcasted_iota(jnp.int32, (ROWS, slots), 1).astype(jnp.float32)
        valid = slot < aux[3, rows, :]
        moved = jnp.where(valid[None], values - mean[None], 0.0)
        departure = jnp.where(valid, aux[0, rows, :] - mean, 0.0)
        high = departure.astype(jnp.bfloat16).astype(jnp.float32)
        rest = jnp.zeros((extra - 2, ROWS, slots), jnp.float32)
        whole = jnp.concatenate([moved, high[None], (departure - high)[None], rest], axis=0)
        turned = jnp.transpose(whole, (1, 0, 2)).astype(jnp.bfloat16)
        for row in range(ROWS):
            dev[chunk, :, row * slots : (row + 1) * slots] = turned[row]

    def products(group, chunk, first):
        start = group * GROUP
        for row in range(ROWS):
            here = slice(row * slots, (row + 1) * slots)
            tile = dev[chunk, 0:members, here]
            for block in range(GROUP):
                line = weight[start + block, chunk, row : row + 1, :]
                line = jnp.broadcast_to(line, (16, slots)).astype(jnp.bfloat16)
                line = jnp.concatenate([line] * (members // 16), axis=0)
                scaled[block * members : (block + 1) * members, here] = tile * line
        product = lax.dot_general(
            scaled[...], dev[chunk], (((1,), (1,)), ((), ())), preferred_element_type=jnp.float32
        )
        product = product.reshape(GROUP, members, members + extra)
        where = pl.ds(start, GROUP)
        if first:
            gram[where, :, 0 : members + extra] = product
        else:
            gram[where, :, 0 : members + extra] += product

    groups = blocks // GROUP

    def over(groups_here, chunk, first):
        def one(index, _):
            products(groups_here(index), chunk, first)
            return 0
        return one

    def outer(index):
        return index + (index // groups) * groups

    gram[...] = jnp.zeros_like(gram)

    def arrive(chunk, _):
        perturb(chunk)
        lax.fori_loop(0, 2 * groups, over(outer, chunk, False), 0)
        return 0

    lax.fori_loop(0, chunks, arrive, 0)
    for side in range(2):
        near_send[side] = gram[pl.ds(2 * side * blocks, blocks)].astype(jnp.bfloat16)
        near_copy(side).start()

    def inside(chunk, _):
        lax.fori_loop(0, groups, over(lambda index: groups + index, chunk, False), 0)
        return 0

    lax.fori_loop(0, chunks, inside, 0)
    for side in range(2):
        near_copy(side).wait()

    total = (
        gram[pl.ds(blocks, blocks)]
        + near_recv[0].astype(jnp.float32)
        + near_recv[1].astype(jnp.float32)
    )
    gram[pl.ds(blocks, blocks)] = total
    share_send[...] = total.reshape(peers, owned, members, LANES).astype(jnp.bfloat16)
    for step in range(1, peers):
        share_copy(step).start()
    ens_own.wait()
    for step in range(1, peers):
        ens_copy(step).wait()
    for step in range(1, peers):
        share_copy(step).wait()

    width = LANES
    line = lax.broadcasted_iota(jnp.int32, (width, width), 0)
    lane = lax.broadcasted_iota(jnp.int32, (width, width), 1)
    eye = jnp.where((line == lane) & (line < members), 1.0, 0.0).astype(jnp.float32)
    square = (line < members) & (lane < members)
    padded = (line // pad) * part + lax.rem(line, pad)
    spread = jnp.where((padded == lane) & (lax.rem(line, pad) < part), 1.0, 0.0).astype(jnp.bfloat16)
    dot = functools.partial(jnp.dot, precision=HIGHEST, preferred_element_type=jnp.float32)

    y_iter, z_iter, bound, push = [], [], [], []
    for own in range(owned):
        part_sum = gram[blocks + mem * owned + own]
        for step in range(1, peers):
            part_sum = part_sum + share_recv[step - 1, own].astype(jnp.float32)
        part_sum = jnp.concatenate(
            [part_sum, jnp.zeros((width - members, LANES), jnp.float32)], axis=0
        )
        forcing = jnp.where((lane == members) | (lane == members + 1), part_sum, 0.0)
        forcing = jnp.sum(forcing, axis=1, keepdims=True)
        system = jnp.where(square, part_sum, 0.0) + (members - 1) / inflation * eye
        sums = jnp.sum(jnp.abs(system), axis=1, keepdims=True)
        most = jnp.max(sums, axis=0, keepdims=True)
        bound.append(most)
        push.append(jnp.broadcast_to(forcing, (width, width)))
        y_iter.append(system / most)
        z_iter.append(eye)
    every = range(owned)
    for sweep in range(NSIT):
        if sweep == 0:
            factor = [1.5 * eye - 0.5 * y_iter[o] for o in every]
            z_iter = factor
        else:
            factor = [1.5 * eye - 0.5 * dot(z_iter[o], y_iter[o]) for o in every]
            z_iter = [dot(factor[o], z_iter[o]) for o in every]
        if sweep < NSIT - 1:
            y_iter = [dot(y_iter[o], factor[o]) for o in every]
    root = [z_iter[o] / jnp.sqrt(bound[o]) for o in every]
    once = [dot(root[o], push[o]) for o in every]
    twice = [dot(root[o], once[o]) for o in every]
    for own in range(owned):
        transform = jnp.where(square, math.sqrt(members - 1) * root[own] + twice[own], 0.0)
        turned = jnp.transpose(transform).astype(jnp.bfloat16)
        turned = jnp.dot(spread, turned, preferred_element_type=jnp.float32).astype(jnp.bfloat16)
        turned = lax.dot_general(
            turned, spread, (((1,), (1,)), ((), ())), preferred_element_type=jnp.float32
        ).astype(jnp.bfloat16)
        state = ens_all[:, own].astype(jnp.float32).reshape(peers * pad, -1)
        mean = jnp.sum(state, axis=0, keepdims=True) / members
        deviation = (state - mean).astype(jnp.bfloat16)
        moved = jnp.dot(turned, deviation, preferred_element_type=jnp.float32)
        analysis = (mean + moved).astype(jnp.bfloat16)
        result[:, own] = analysis.reshape(peers, pad, -1)

    for step in range(1, peers):
        out_copy(step).start()
    out_own = pltpu.make_async_copy(
        result.at[mem], out_ref.at[pl.ds(mem * owned, owned)], local_sem.at[0]
    )
    out_own.start()
    out_own.wait()
    for step in range(1, peers):
        out_copy(step).wait()


def per_device(ens_state, obs_prior, obs_value, obs_prec, obs_len, pair_block, obs_pos):
    peers = lax.axis_size("mem")
    ring = lax.axis_size("grid")
    part, blocks, length = ens_state.shape
    members = peers * part
    slots = obs_prior.shape[2]
    share = obs_prior.shape[1] // peers
    chunks = share // ROWS
    owned = blocks // peers
    pad = LANES // peers
    extra = 16
    dims = (peers, ring, part, chunks, owned, blocks, members, pad, extra)

    ens = jnp.pad(jnp.transpose(ens_state, (1, 0, 2)), ((0, 0), (0, pad - part), (0, 0)))
    counts = jnp.broadcast_to(obs_len.astype(jnp.float32)[:, None], obs_value.shape)
    aux = jnp.stack([obs_value, obs_prec, obs_pos, counts])

    bf16, f32 = jnp.bfloat16, jnp.float32
    others = peers - 1
    dma = pltpu.SemaphoreType.DMA
    anywhere = pl.BlockSpec(memory_space=pl.ANY)
    out = pl.pallas_call(
        functools.partial(kernel, dims),
        out_shape=jax.ShapeDtypeStruct((blocks, pad, length), bf16),
        in_specs=[anywhere] * 4,
        out_specs=anywhere,
        scratch_shapes=[
            pltpu.VMEM((chunks, members, ROWS, slots), bf16),
            pltpu.VMEM((chunks, members + extra, ROWS * slots), bf16),
            pltpu.VMEM((3 * blocks, chunks, ROWS, slots), f32),
            pltpu.VMEM((4, share, slots), f32),
            pltpu.VMEM((3,) + pair_block.shape, jnp.int32),
            pltpu.VMEM((GROUP * members, ROWS * slots), bf16),
            pltpu.VMEM((3 * blocks, members, LANES), f32),
            pltpu.VMEM((2, blocks, members, LANES), bf16),
            pltpu.VMEM((2, blocks, members, LANES), bf16),
            pltpu.VMEM((peers, owned, members, LANES), bf16),
            pltpu.VMEM((others, owned, members, LANES), bf16),
            pltpu.VMEM((peers, owned, pad, length), bf16),
            pltpu.VMEM((peers, owned, pad, length), bf16),
            dma((3 + chunks,)),
            dma((chunks, others)),
            dma((chunks, others)),
            dma((others,)),
            dma((others,)),
            dma((2,)),
            dma((2,)),
            dma((2,)),
            dma((2,)),
            dma((others,)),
            dma((others,)),
            dma((others,)),
            dma((others,)),
        ],
        compiler_params=pltpu.CompilerParams(
            collective_id=0, has_side_effects=True, vmem_limit_bytes=48 * 2**20
        ),
    )(ens, obs_prior, aux, pair_block)
    return jnp.transpose(out[:, :part, :], (1, 0, 2))


def solution(mesh):
    placed = (
        P("mem", "grid", None),
        P("mem", "grid", None),
        P("grid", None),
        P("grid", None),
        P("grid"),
        P("grid", None),
        P("grid", None),
    )
    return jax.shard_map(
        per_device, mesh=mesh, in_specs=placed, out_specs=P("mem", "grid", None), check_vma=False
    )
```
